128 devices in a mesh: row: 8 (over y, x_hi), col: 16 (over z, x_lo, core).
Axes of the slice: x: 4 (x_hi: 2, x_lo: 2; x = x_hi * 2 + x_lo), y: 4, z: 4, core: 2. Of those that a mesh axis runs over, the one named last changes fastest.
Arguments:
- right_sides: bfloat16 [64, 2097152], P(None, ('row', 'col')), may hold values from -6 to 6
- leaf_factor: bfloat16 [16384, 64, 128], P(('row', 'col')), may hold values from -0.5 to 0.5
- middle_factor: bfloat16 [8, 16384, 64, 128], P(None, ('row', 'col')), may hold values from -0.5 to 0.5
- root_factor: bfloat16 [16384, 64, 128], P(('row', 'col')), may hold values from -0.75 to 0.75
- partners: int32 [8, 128, 128], P(None, ('row', 'col')), may hold values from 0 to 127, each once within a row
- pattern: int32 [8, 128, 128], P(None, ('row', 'col')), may hold values 0 or 1
Outputs:
- applied: bfloat16 [64, 2097152], P(None, ('row', 'col'))
The draws below stay inside these ranges and needn't reach their ends.
Inputs may be any that keep to these rules, and one draw needn't show every extreme that they name: partners[l, d, :] is a permutation of 0 .. 127 for every level and device.
All inputs are finite; a program needn't handle non-finite values. No bound on the sum of `pattern` on one device may be relied on, other than what follows from the above.
Results may differ from the reference program's by a relative error of at most 0.017.
Values may be sent and summed in bfloat16 or wider, within the bound.
A program may use at most 128 MiB of HBM per device.

```python
import jax
import jax.numpy as jnp

NRHS = 64
RANK = 64
LEAF = 128
BLK_DEV = 128
LOCAL_LEV = 1
ROW_LEV = 3
COL_LEV = 4
LEVELS = 8
NBLK = 16384
N_ROW = 8
N_COL = 16
DEVICES = 128


def with_ends(drawn, stream_key, least, high):
    shape = drawn.shape
    spot = [jax.random.randint(jax.random.fold_in(stream_key, axis), (), 0, shape[axis]) for axis in range(len(shape))]
    drawn = drawn.at[tuple(spot)].set(least)
    longest = shape.index(max(shape))
    spot[longest] = (spot[longest] + 1) % shape[longest]
    return drawn.at[tuple(spot)].set(high)


def steps_of(own_key, shape, pieces, smallest, largest):
    loudness = 1.0
    for axis_at, shards_of in pieces:
        draws = jax.random.uniform(jax.random.fold_in(jax.random.fold_in(own_key, 6), axis_at), (shards_of,), jnp.float32, smallest / len(pieces), largest / len(pieces))
        loudness = loudness * jnp.repeat(jnp.exp(draws), shape[axis_at] // shards_of).reshape((-1,) + (1,) * (len(shape) - 1 - axis_at))
    return loudness


def centred(stream_key, dims, scale, most, shards=(), kind=jnp.bfloat16):
    array = jax.random.normal(stream_key, dims, jnp.float32) * scale
    if len(shards) > 0:
        array = steps_of(stream_key, dims, shards, -0.22, 0.18) * array
    return jnp.clip(array, min=-most, max=most).astype(kind)


def setup_inputs(seed: int = 0) -> dict:
    seeds = jax.random.split(jax.random.key(seed), 7)
    return {
        "right_sides": centred(seeds[0], (NRHS, NBLK * LEAF), 1.0, 6.0, ((1, 128),)),
        "leaf_factor": centred(seeds[1], (NBLK, RANK, LEAF), LEAF ** -0.5, 0.5, ((0, 128),)),
        "middle_factor": centred(seeds[2], (LEVELS, NBLK, RANK, 2 * RANK), (2 * RANK) ** -0.5, 0.5, ((1, 128),)),
        "root_factor": centred(seeds[3], (NBLK, RANK, LEAF), RANK ** -0.5, 0.75, ((0, 128),)),
        "partners": jax.vmap(lambda own: jax.random.permutation(own, BLK_DEV))(jax.random.split(seeds[4], LEVELS * DEVICES)).reshape((LEVELS, DEVICES, BLK_DEV)).astype(jnp.int32),
        "pattern": with_ends((jax.random.randint(seeds[5], (LEVELS, DEVICES, BLK_DEV), 0, 4) < 3).astype(jnp.int32), jax.random.fold_in(seeds[5], 1), 0, 1),
    }


def mix_level(state, other, weights, order, keep):
    rows = jnp.arange(N_ROW)[:, None, None]
    cols = jnp.arange(N_COL)[None, :, None]
    picked = other[rows, cols, order].astype(jnp.float32)
    picked = picked * keep.astype(jnp.float32)[..., None, None]
    joined = jnp.concatenate([state.astype(jnp.float32), picked], axis=-1)
    result = jnp.einsum('rcbnk,rcbik->rcbni', joined, weights.astype(jnp.float32))
    return result.astype(jnp.bfloat16)


def reference(right_sides, leaf_factor, middle_factor, root_factor, partners, pattern):
    inputs = right_sides.astype(jnp.float32).reshape(NRHS, NBLK, LEAF)
    state = jnp.einsum('nbp,bip->bni', inputs, leaf_factor.astype(jnp.float32)).astype(jnp.bfloat16)
    state = state.reshape(N_ROW, N_COL, BLK_DEV, NRHS, RANK)
    order = partners.reshape(LEVELS, N_ROW, N_COL, BLK_DEV)
    keep = pattern.reshape(LEVELS, N_ROW, N_COL, BLK_DEV)
    weights = middle_factor.reshape(LEVELS, N_ROW, N_COL, BLK_DEV, RANK, 2 * RANK)
    level = 0
    for step in range(LOCAL_LEV):
        state = mix_level(state, state, weights[level], order[level], keep[level])
        level = level + 1
    for bit in range(ROW_LEV):
        flipped = jnp.bitwise_xor(jnp.arange(N_ROW), 1 << bit)
        state = mix_level(state, state[flipped], weights[level], order[level], keep[level])
        level = level + 1
    group = BLK_DEV // N_COL
    state = state.reshape(N_ROW, N_COL, N_COL, group, NRHS, RANK)
    state = jnp.swapaxes(state, 1, 2).reshape(N_ROW, N_COL, BLK_DEV, NRHS, RANK)
    for bit in range(COL_LEV):
        flipped = jnp.bitwise_xor(jnp.arange(N_COL), 1 << bit)
        state = mix_level(state, state[:, flipped], weights[level], order[level], keep[level])
        level = level + 1
    state = state.reshape(NBLK, NRHS, RANK).astype(jnp.float32)
    result = jnp.einsum('bni,bip->nbp', state, root_factor.astype(jnp.float32))
    return result.astype(jnp.bfloat16).reshape(NRHS, NBLK * LEAF)
```

```python
import functools

import jax
import jax.numpy as jnp
from jax import lax
from jax.experimental import pallas as pl
from jax.experimental.pallas import tpu as pltpu
from jax.sharding import PartitionSpec as P

MESH = pl.DeviceIdType.MESH
BF16, F32 = jnp.bfloat16, jnp.float32
CHUNKS = (16, 16, 16, 16)
GROUP = 16
SKEW = 1


def dot_t(a, b):
    return lax.dot_general(a, b, (((1,), (1,)), ((), ())), preferred_element_type=F32)


def task_order(chunks, stages, skew):
    order = []
    for t in range(stages + (chunks - 1) * skew):
        for k in range(chunks):
            if 0 <= t - k * skew < stages:
                order.append((k, t - k * skew))
    return order


def kernel(row_bits, col_bits, chunks, order, *refs):
    refs = list(refs)
    part, pat, x_hbm, leaf_hbm, mid_hbm, root_hbm, out_hbm = refs[:7]
    x, leaf, mid, root, out = refs[7:12]
    x_sem, w_sem, out_sem, send_sem, recv_sem = refs[12:17]
    rest = iter(refs[17:])
    n_chunks = len(chunks)
    starts = [sum(chunks[:k]) for k in range(n_chunks)]
    levels = row_bits + col_bits + 1
    t_stage = row_bits + 1
    first = [next(rest) for _ in chunks]
    state = [[next(rest), next(rest)] for _ in chunks]
    moved = [next(rest) for _ in chunks]
    got = [
        {s: next(rest) for s in range(1, levels + 1) if s != t_stage} for _ in chunks
    ]
    pairs = leaf.shape[0]
    cols = 1 << col_bits
    band = pairs // cols
    r, c = lax.axis_index("row"), lax.axis_index("col")

    def peer(s):
        if s < t_stage:
            return (r ^ (1 << (s - 1)), c)
        return (r, c ^ (1 << (s - t_stage - 1)))

    def rows(k):
        return pl.ds(starts[k], chunks[k])

    def x_copy(k):
        return pltpu.make_async_copy(x_hbm.at[rows(k)], x.at[rows(k)], x_sem.at[k])

    def out_copy(k):
        return pltpu.make_async_copy(
            out.at[rows(k)], out_hbm.at[rows(k)], out_sem.at[k]
        )

    leaf_copy = pltpu.make_async_copy(leaf_hbm, leaf, w_sem.at[levels])
    root_copy = pltpu.make_async_copy(root_hbm, root, w_sem.at[levels + 1])

    def mid_copy(l):
        return pltpu.make_async_copy(mid_hbm.at[l], mid.at[l], w_sem.at[l])

    x_copy(0).start()
    leaf_copy.start()
    mid_copy(0).start()
    for k in range(1, n_chunks):
        x_copy(k).start()
    for l in range(1, levels):
        mid_copy(l).start()
    root_copy.start()

    barrier = pltpu.get_barrier_semaphore()
    for s in range(1, t_stage):
        pl.semaphore_signal(barrier, inc=1, device_id=peer(s), device_id_type=MESH)
    for d in range(1, cols):
        pl.semaphore_signal(barrier, inc=1, device_id=(r, c ^ d), device_id_type=MESH)

    for k in range(n_chunks):
        blank = jnp.zeros((chunks[k], 128), BF16)
        first[k][pairs] = blank
        for s in got[k]:
            got[k][s][pairs] = blank

    def send(k, s, source, at, count):
        return pltpu.make_async_remote_copy(
            src_ref=source.at[pl.ds(at, count)],
            dst_ref=got[k][s].at[pl.ds(at, count)],
            send_sem=send_sem.at[k, s],
            recv_sem=recv_sem.at[k, s],
            device_id=peer(s),
            device_id_type=MESH,
        )

    def move(k, source, d):
        j = c ^ d
        return pltpu.make_async_remote_copy(
            src_ref=source.at[pl.ds(j * band, band)],
            dst_ref=moved[k].at[pl.ds(c * band, band)],
            send_sem=send_sem.at[k, t_stage],
            recv_sem=recv_sem.at[k, t_stage],
            device_id=(r, j),
            device_id_type=MESH,
        )

    def moved_all(k, source):
        count = pairs - band
        return pltpu.make_async_remote_copy(
            src_ref=source.at[pl.ds(0, count)],
            dst_ref=moved[k].at[pl.ds(0, count)],
            send_sem=send_sem.at[k, t_stage],
            recv_sem=recv_sem.at[k, t_stage],
            device_id=(r, c ^ 1),
            device_id_type=MESH,
        )

    def low(k):
        return lax.broadcasted_iota(jnp.int32, (chunks[k], 128), 1) < 64

    def grouped(body, after=None):
        def step(g, carry):
            at = g * GROUP
            body([at + i for i in range(GROUP)])
            if after is not None:
                after(at)
            return carry

        lax.fori_loop(0, pairs // GROUP, step, 0)

    def leaf_task(k):
        n, half = chunks[k], low(k)

        def body(qs):
            ys = []
            for q in qs:
                both = x[rows(k), pl.ds(pl.multiple_of(q * 256, 256), 256)]
                z = jnp.concatenate([both[:, :128], both[:, 128:]], axis=0)
                ys.append(dot_t(z, leaf[q]))
            for q, y in zip(qs, ys):
                first[k][q] = jnp.where(half, y[:n], y[n:]).astype(BF16)

        grouped(body)

    def level_task(k, l, own, other, result, after):
        n, half = chunks[k], low(k)

        def picked(b):
            p, keep = part[l, b], pat[l, b]
            tile = pairs + keep * ((p >> 1) - pairs)
            turn = 1 - (p & 1)
            return pltpu.roll(other[tile], turn * 64, 1)

        def body(qs):
            ys = []
            for q in qs:
                mine = own[q]
                even = jnp.where(half, mine, picked(2 * q))
                odd = jnp.where(half, pltpu.roll(mine, 64, 1), picked(2 * q + 1))
                ys.append(dot_t(jnp.concatenate([even, odd], axis=0), mid[l, q]))
            for q, y in zip(qs, ys):
                result[q] = jnp.where(half, y[:n], y[n:]).astype(BF16)

        grouped(body, after)

    def root_task(k, source):
        n, half = chunks[k], low(k)

        def body(qs):
            ys = []
            for q in qs:
                mine = source[q]
                none = jnp.zeros_like(mine)
                z = jnp.concatenate(
                    [jnp.where(half, mine, none), jnp.where(half, none, mine)], axis=0
                )
                ys.append(jnp.dot(z, root[q], preferred_element_type=F32))
            for q, y in zip(qs, ys):
                y = y.astype(BF16)
                at = pl.multiple_of(q * 256, 256)
                out[rows(k), pl.ds(at, 128)] = y[:n]
                out[rows(k), pl.ds(at + 128, 128)] = y[n:]

        grouped(body)

    ready = set()

    def need(name, copy):
        if name not in ready:
            ready.add(name)
            copy().wait()

    greeted = [False]

    def greet():
        if not greeted[0]:
            greeted[0] = True
            pl.semaphore_wait(barrier, row_bits + cols - 1)

    def sender(k, s, source):
        def after(at):
            send(k, s, source, at, GROUP).start()

        return after

    held = {}
    for k, t in order:
        if t == 0:
            need(("x", k), lambda: x_copy(k))
            need("leaf", lambda: leaf_copy)
            leaf_task(k)
            need(("mid", 0), lambda: mid_copy(0))
            greet()
            level_task(k, 0, first[k], first[k], state[k][0], sender(k, 1, state[k][0]))
            held[k] = state[k][0]
        elif t == t_stage:
            moved_all(k, held[k]).wait_recv()
            held[k] = moved[k]
            send(k, t + 1, moved[k], 0, pairs).start()
        elif t <= levels:
            l = t if t < t_stage else t - 1
            need(("mid", l), lambda: mid_copy(l))
            send(k, t, held[k], 0, pairs).wait_recv()
            result = state[k][l % 2]
            if l >= 2:
                before = l - 1 if l <= t_stage + 1 else l
                if before == t_stage:
                    moved_all(k, result).wait_send()
                else:
                    send(k, before, result, 0, pairs).wait_send()
            if t == t_stage - 1:
                level_task(k, l, held[k], got[k][t], result, None)
                for d in range(1, cols):
                    move(k, result, d).start()
                moved[k][pl.ds(c * band, band)] = result[pl.ds(c * band, band)]
            elif t == levels:
                level_task(k, l, held[k], got[k][t], result, None)
            else:
                level_task(k, l, held[k], got[k][t], result, sender(k, t + 1, result))
            held[k] = result
        else:
            need("root", lambda: root_copy)
            root_task(k, held[k])
            out_copy(k).start()
    for k in range(n_chunks):
        send(k, t_stage + 1, moved[k], 0, pairs).wait_send()
        send(k, levels, state[k][0], 0, pairs).wait_send()
        out_copy(k).wait()


def per_device(right_sides, leaf_factor, middle_factor, root_factor, partners, pattern):
    row_bits = lax.axis_size("row").bit_length() - 1
    col_bits = lax.axis_size("col").bit_length() - 1
    nrhs = right_sides.shape[0]
    blocks, rank, width = leaf_factor.shape
    pairs, levels = blocks // 2, middle_factor.shape[0]
    chunks = CHUNKS
    t_stage = row_bits + 1
    stages = [s for s in range(1, levels + 1) if s != t_stage]
    tiles = [
        pltpu.VMEM((pairs + 1, n, width), BF16) for n in chunks
    ]
    plain = [pltpu.VMEM((pairs, n, width), BF16) for n in chunks]
    scratch = [
        pltpu.VMEM((nrhs, blocks * width), BF16),
        pltpu.VMEM((pairs, 2 * rank, width), BF16),
        pltpu.VMEM((levels, pairs, 2 * rank, width), BF16),
        pltpu.VMEM((pairs, 2 * rank, width), BF16),
        pltpu.VMEM((nrhs, blocks * width), BF16),
        pltpu.SemaphoreType.DMA((len(chunks),)),
        pltpu.SemaphoreType.DMA((levels + 2,)),
        pltpu.SemaphoreType.DMA((len(chunks),)),
        pltpu.SemaphoreType.DMA((len(chunks), levels + 1)),
        pltpu.SemaphoreType.DMA((len(chunks), levels + 1)),
    ]
    scratch += tiles
    for one in plain:
        scratch += [one, one]
    scratch += plain
    for one in tiles:
        scratch += [one] * len(stages)
    order = task_order(len(chunks), levels + 2, SKEW)
    anywhere = pl.BlockSpec(memory_space=pl.ANY)
    scalars = pl.BlockSpec(memory_space=pltpu.SMEM)
    return pl.pallas_call(
        functools.partial(kernel, row_bits, col_bits, chunks, order),
        out_shape=jax.ShapeDtypeStruct(right_sides.shape, BF16),
        in_specs=[scalars, scalars] + [anywhere] * 4,
        out_specs=anywhere,
        scratch_shapes=scratch,
        compiler_params=pltpu.CompilerParams(
            collective_id=0, has_side_effects=True, vmem_limit_bytes=58 << 20
        ),
    )(
        partners.reshape(levels, blocks),
        pattern.reshape(levels, blocks),
        right_sides,
        leaf_factor.reshape(pairs, 2 * rank, width),
        middle_factor.reshape(levels, pairs, 2 * rank, width),
        root_factor.reshape(pairs, 2 * rank, width),
    )


def solution(mesh):
    in_specs = (
        P(None, ("row", "col")),
        P(("row", "col"), None, None),
        P(None, ("row", "col"), None, None),
        P(("row", "col"), None, None),
        P(None, ("row", "col"), None),
        P(None, ("row", "col"), None),
    )
    out_specs = P(None, ("row", "col"))
    return jax.shard_map(
        per_device, mesh=mesh, in_specs=in_specs, out_specs=out_specs, check_vma=False
    )
```

```python
import functools

import jax
import jax.numpy as jnp
from jax import lax
from jax.experimental import pallas as pl
from jax.experimental.pallas import tpu as pltpu
from jax.sharding import PartitionSpec as P

MESH = pl.DeviceIdType.MESH
BF16, F32 = jnp.bfloat16, jnp.float32
CHUNKS = (16, 16, 16, 16)
GROUP = 32
ORDER = (
    (0, 0), (0, 1), (1, 0), (3, 0), (0, 2), (2, 0), (1, 1), (0, 3),
    (1, 2), (0, 4), (2, 1), (0, 5), (1, 3), (3, 1), (0, 6), (2, 2),
    (1, 4), (1, 5), (0, 7), (3, 2), (2, 3), (1, 6), (3, 3), (2, 4),
    (2, 5), (1, 7), (3, 4), (3, 5), (2, 6), (1, 8), (3, 6), (2, 7),
    (1, 9), (3, 7), (0, 8), (2, 8), (2, 9), (0, 9), (3, 8), (3, 9),
)


def wide(zs, weights, contract):
    out = []
    for i in range(0, len(zs), 2):
        both = jnp.concatenate(weights[i : i + 2], axis=1 - contract)
        y = lax.dot_general(
            jnp.concatenate(zs[i : i + 2], axis=0),
            both,
            (((1,), (contract,)), ((), ())),
            preferred_element_type=F32,
        )
        rows = zs[i].shape[0]
        out += [y[:rows, :128], y[rows:, 128:]]
    return out


def kernel(row_bits, col_bits, chunks, order, *refs):
    refs = list(refs)
    part, pat, x_hbm, leaf_hbm, mid_hbm, root_hbm, out_hbm = refs[:7]
    x, leaf, mid, root, out = refs[7:12]
    x_sem, w_sem, out_sem, send_sem, recv_sem = refs[12:17]
    rest = iter(refs[17:])
    n_chunks = len(chunks)
    starts = [sum(chunks[:k]) for k in range(n_chunks)]
    levels = row_bits + col_bits + 1
    t_stage = row_bits + 1
    first = [next(rest) for _ in chunks]
    state = [[next(rest), next(rest)] for _ in chunks]
    moved = [next(rest) for _ in chunks]
    got = [
        {s: next(rest) for s in range(1, levels + 1) if s != t_stage} for _ in chunks
    ]
    pairs = leaf.shape[0]
    cols = 1 << col_bits
    band = pairs // cols
    r, c = lax.axis_index("row"), lax.axis_index("col")

    def peer(s):
        if s < t_stage:
            return (r ^ (1 << (s - 1)), c)
        return (r, c ^ (1 << (s - t_stage - 1)))

    def rows(k):
        return pl.ds(starts[k], chunks[k])

    def x_copy(k):
        return pltpu.make_async_copy(x_hbm.at[rows(k)], x.at[rows(k)], x_sem.at[k])

    def out_copy(k):
        return pltpu.make_async_copy(
            out.at[rows(k)], out_hbm.at[rows(k)], out_sem.at[k]
        )

    leaf_copy = pltpu.make_async_copy(leaf_hbm, leaf, w_sem.at[levels])
    root_copy = pltpu.make_async_copy(root_hbm, root, w_sem.at[levels + 1])

    def mid_copy(l):
        return pltpu.make_async_copy(mid_hbm.at[l], mid.at[l], w_sem.at[l])

    x_copy(0).start()
    leaf_copy.start()
    mid_copy(0).start()
    for k in range(1, n_chunks):
        x_copy(k).start()
    for l in range(1, levels):
        mid_copy(l).start()
    root_copy.start()

    barrier = pltpu.get_barrier_semaphore()
    for s in range(1, t_stage):
        pl.semaphore_signal(barrier, inc=1, device_id=peer(s), device_id_type=MESH)
    for d in range(1, cols):
        pl.semaphore_signal(barrier, inc=1, device_id=(r, c ^ d), device_id_type=MESH)

    for k in range(n_chunks):
        blank = jnp.zeros((chunks[k], 128), BF16)
        first[k][pairs] = blank
        for s in got[k]:
            got[k][s][pairs] = blank

    def send(k, s, source, at, count):
        return pltpu.make_async_remote_copy(
            src_ref=source.at[pl.ds(at, count)],
            dst_ref=got[k][s].at[pl.ds(at, count)],
            send_sem=send_sem.at[k, s],
            recv_sem=recv_sem.at[k, s],
            device_id=peer(s),
            device_id_type=MESH,
        )

    def move(k, source, d):
        j = c ^ d
        return pltpu.make_async_remote_copy(
            src_ref=source.at[pl.ds(j * band, band)],
            dst_ref=moved[k].at[pl.ds(c * band, band)],
            send_sem=send_sem.at[k, t_stage],
            recv_sem=recv_sem.at[k, t_stage],
            device_id=(r, j),
            device_id_type=MESH,
        )

    def moved_all(k, source):
        count = pairs - band
        return pltpu.make_async_remote_copy(
            src_ref=source.at[pl.ds(0, count)],
            dst_ref=moved[k].at[pl.ds(0, count)],
            send_sem=send_sem.at[k, t_stage],
            recv_sem=recv_sem.at[k, t_stage],
            device_id=(r, c ^ 1),
            device_id_type=MESH,
        )

    def low(k):
        return lax.broadcasted_iota(jnp.int32, (chunks[k], 128), 1) < 64

    def grouped(body, after=None):
        def step(g, carry):
            at = g * GROUP
            body([at + i for i in range(GROUP)])
            if after is not None:
                after(at)
            return carry

        lax.fori_loop(0, pairs // GROUP, step, 0)

    def leaf_task(k):
        n, half = chunks[k], low(k)

        def body(qs):
            zs = []
            for q in qs:
                both = x[rows(k), pl.ds(pl.multiple_of(q * 256, 256), 256)]
                zs.append(jnp.concatenate([both[:, :128], both[:, 128:]], axis=0))
            ys = wide(zs, [leaf[q] for q in qs], 1)
            for q, y in zip(qs, ys):
                first[k][q] = jnp.where(half, y[:n], y[n:]).astype(BF16)

        grouped(body)

    def level_task(k, l, own, other, result, after):
        n, half = chunks[k], low(k)

        def picked(b):
            p, keep = part[l, b], pat[l, b]
            tile = pairs + keep * ((p >> 1) - pairs)
            turn = 1 - (p & 1)
            return pltpu.roll(other[tile], turn * 64, 1)

        def body(qs):
            zs = []
            for q in qs:
                mine = own[q]
                even = jnp.where(half, mine, picked(2 * q))
                odd = jnp.where(half, pltpu.roll(mine, 64, 1), picked(2 * q + 1))
                zs.append(jnp.concatenate([even, odd], axis=0))
            ys = wide(zs, [mid[l, q] for q in qs], 1)
            for q, y in zip(qs, ys):
                result[q] = jnp.where(half, y[:n], y[n:]).astype(BF16)

        grouped(body, after)

    def root_task(k, source):
        n, half = chunks[k], low(k)

        def body(qs):
            zs = []
            for q in qs:
                mine = source[q]
                none = jnp.zeros_like(mine)
                z = [jnp.where(half, mine, none), jnp.where(half, none, mine)]
                zs.append(jnp.concatenate(z, axis=0))
            ys = wide(zs, [root[q] for q in qs], 0)
            for q, y in zip(qs, ys):
                y = y.astype(BF16)
                at = pl.multiple_of(q * 256, 256)
                out[rows(k), pl.ds(at, 128)] = y[:n]
                out[rows(k), pl.ds(at + 128, 128)] = y[n:]

        grouped(body)

    ready = set()

    def need(name, copy):
        if name not in ready:
            ready.add(name)
            copy().wait()

    greeted = [False]

    def greet():
        if not greeted[0]:
            greeted[0] = True
            pl.semaphore_wait(barrier, row_bits + cols - 1)

    def sender(k, s, source):
        def after(at):
            send(k, s, source, at, GROUP).start()

        return after

    held = {}
    for k, t in order:
        if t == 0:
            need(("x", k), lambda: x_copy(k))
            need("leaf", lambda: leaf_copy)
            leaf_task(k)
            need(("mid", 0), lambda: mid_copy(0))
            greet()
            level_task(k, 0, first[k], first[k], state[k][0], sender(k, 1, state[k][0]))
            held[k] = state[k][0]
        elif t == t_stage:
            moved_all(k, held[k]).wait_recv()
            held[k] = moved[k]
            send(k, t + 1, moved[k], 0, pairs).start()
        elif t <= levels:
            l = t if t < t_stage else t - 1
            need(("mid", l), lambda: mid_copy(l))
            send(k, t, held[k], 0, pairs).wait_recv()
            result = state[k][l % 2]
            if l >= 2:
                before = l - 1 if l <= t_stage + 1 else l
                if before == t_stage:
                    moved_all(k, result).wait_send()
                else:
                    send(k, before, result, 0, pairs).wait_send()
            if t == t_stage - 1:
                level_task(k, l, held[k], got[k][t], result, None)
                for d in range(1, cols):
                    move(k, result, d).start()
                moved[k][pl.ds(c * band, band)] = result[pl.ds(c * band, band)]
            elif t == levels:
                level_task(k, l, held[k], got[k][t], result, None)
            else:
                level_task(k, l, held[k], got[k][t], result, sender(k, t + 1, result))
            held[k] = result
        else:
            need("root", lambda: root_copy)
            root_task(k, held[k])
            out_copy(k).start()
    for k in range(n_chunks):
        send(k, t_stage + 1, moved[k], 0, pairs).wait_send()
        send(k, levels, state[k][0], 0, pairs).wait_send()
        out_copy(k).wait()


def per_device(right_sides, leaf_factor, middle_factor, root_factor, partners, pattern):
    row_bits = lax.axis_size("row").bit_length() - 1
    col_bits = lax.axis_size("col").bit_length() - 1
    nrhs = right_sides.shape[0]
    blocks, rank, width = leaf_factor.shape
    pairs, levels = blocks // 2, middle_factor.shape[0]
    chunks = CHUNKS
    t_stage = row_bits + 1
    stages = [s for s in range(1, levels + 1) if s != t_stage]
    tiles = [
        pltpu.VMEM((pairs + 1, n, width), BF16) for n in chunks
    ]
    plain = [pltpu.VMEM((pairs, n, width), BF16) for n in chunks]
    scratch = [
        pltpu.VMEM((nrhs, blocks * width), BF16),
        pltpu.VMEM((pairs, 2 * rank, width), BF16),
        pltpu.VMEM((levels, pairs, 2 * rank, width), BF16),
        pltpu.VMEM((pairs, 2 * rank, width), BF16),
        pltpu.VMEM((nrhs, blocks * width), BF16),
        pltpu.SemaphoreType.DMA((len(chunks),)),
        pltpu.SemaphoreType.DMA((levels + 2,)),
        pltpu.SemaphoreType.DMA((len(chunks),)),
        pltpu.SemaphoreType.DMA((len(chunks), levels + 1)),
        pltpu.SemaphoreType.DMA((len(chunks), levels + 1)),
    ]
    scratch += tiles
    for one in plain:
        scratch += [one, one]
    scratch += plain
    for one in tiles:
        scratch += [one] * len(stages)
    order = ORDER
    anywhere = pl.BlockSpec(memory_space=pl.ANY)
    scalars = pl.BlockSpec(memory_space=pltpu.SMEM)
    return pl.pallas_call(
        functools.partial(kernel, row_bits, col_bits, chunks, order),
        out_shape=jax.ShapeDtypeStruct(right_sides.shape, BF16),
        in_specs=[scalars, scalars] + [anywhere] * 4,
        out_specs=anywhere,
        scratch_shapes=scratch,
        compiler_params=pltpu.CompilerParams(
            collective_id=0, has_side_effects=True, vmem_limit_bytes=58 << 20
        ),
    )(
        partners.reshape(levels, blocks),
        pattern.reshape(levels, blocks),
        right_sides,
        leaf_factor.reshape(pairs, 2 * rank, width),
        middle_factor.reshape(levels, pairs, 2 * rank, width),
        root_factor.reshape(pairs, 2 * rank, width),
    )


def solution(mesh):
    in_specs = (
        P(None, ("row", "col")),
        P(("row", "col"), None, None),
        P(None, ("row", "col"), None, None),
        P(("row", "col"), None, None),
        P(None, ("row", "col"), None),
        P(None, ("row", "col"), None),
    )
    out_specs = P(None, ("row", "col"))
    return jax.shard_map(
        per_device, mesh=mesh, in_specs=in_specs, out_specs=out_specs, check_vma=False
    )
```

```python
import functools

import jax
import jax.numpy as jnp
from jax import lax
from jax.experimental import pallas as pl
from jax.experimental.pallas import tpu as pltpu
from jax.sharding import PartitionSpec as P

MESH = pl.DeviceIdType.MESH
BF16, F32 = jnp.bfloat16, jnp.float32
CHUNKS = (8, 8, 16, 16, 8, 8)
GROUP = 32
ORDER = (
    (1, 0), (0, 0), (2, 0), (4, 0), (1, 1), (0, 1), (1, 2), (5, 0),
    (2, 1), (0, 2), (1, 3), (3, 0), (2, 2), (5, 1), (1, 4), (4, 1),
    (0, 3), (1, 5), (2, 3), (0, 4), (0, 5), (5, 2), (1, 6), (3, 1),
    (2, 4), (0, 6), (5, 3), (2, 5), (4, 2), (1, 7), (0, 7), (3, 2),
    (4, 3), (2, 6), (1, 8), (3, 3), (4, 4), (4, 5), (2, 7), (5, 4),
    (5, 5), (0, 8), (1, 9), (3, 4), (4, 6), (3, 5), (2, 8), (5, 6),
    (2, 9), (0, 9), (4, 7), (3, 6), (5, 7), (3, 7), (4, 8), (5, 8),
    (4, 9), (5, 9), (3, 8), (3, 9),
)


def wide(zs, weights, contract):
    out = []
    for i in range(0, len(zs), 2):
        both = jnp.concatenate(weights[i : i + 2], axis=1 - contract)
        y = lax.dot_general(
            jnp.concatenate(zs[i : i + 2], axis=0),
            both,
            (((1,), (contract,)), ((), ())),
            preferred_element_type=F32,
        )
        rows = zs[i].shape[0]
        out += [y[:rows, :128], y[rows:, 128:]]
    return out


def kernel(row_bits, col_bits, chunks, order, *refs):
    refs = list(refs)
    part, pat, x_hbm, leaf_hbm, mid_hbm, root_hbm, out = refs[:7]
    x, leaf, mid, root = refs[7:11]
    x_sem, w_sem, send_sem, recv_sem = refs[11:15]
    rest = iter(refs[15:])
    n_chunks = len(chunks)
    starts = [sum(chunks[:k]) for k in range(n_chunks)]
    levels = row_bits + col_bits + 1
    t_stage = row_bits + 1
    first = [next(rest) for _ in chunks]
    state = [[next(rest), next(rest)] for _ in chunks]
    moved = [next(rest) for _ in chunks]
    got = [
        {s: next(rest) for s in range(1, levels + 1) if s != t_stage} for _ in chunks
    ]
    pairs = leaf.shape[0]
    cols = 1 << col_bits
    band = pairs // cols
    r, c = lax.axis_index("row"), lax.axis_index("col")

    def peer(s):
        if s < t_stage:
            return (r ^ (1 << (s - 1)), c)
        return (r, c ^ (1 << (s - t_stage - 1)))

    def rows(k):
        return pl.ds(starts[k], chunks[k])

    n_bands = sum(chunks) // 16

    def bands(k):
        return range(starts[k] // 16, (starts[k] + chunks[k] - 1) // 16 + 1)

    def x_copy(i):
        at = pl.ds(i * 16, 16)
        return pltpu.make_async_copy(x_hbm.at[at], x.at[at], x_sem.at[i])

    leaf_copy = pltpu.make_async_copy(leaf_hbm, leaf, w_sem.at[levels])
    root_copy = pltpu.make_async_copy(root_hbm, root, w_sem.at[levels + 1])

    def mid_copy(l):
        return pltpu.make_async_copy(mid_hbm.at[l], mid.at[l], w_sem.at[l])

    x_first = order[0][0]
    for i in bands(x_first):
        x_copy(i).start()
    leaf_copy.start()
    mid_copy(0).start()
    for i in range(n_bands):
        if i not in bands(x_first):
            x_copy(i).start()
    for l in range(1, levels):
        mid_copy(l).start()
    root_copy.start()

    barrier = pltpu.get_barrier_semaphore()
    for s in range(1, t_stage):
        pl.semaphore_signal(barrier, inc=1, device_id=peer(s), device_id_type=MESH)
    for d in range(1, cols):
        pl.semaphore_signal(barrier, inc=1, device_id=(r, c ^ d), device_id_type=MESH)

    for k in range(n_chunks):
        blank = jnp.zeros((chunks[k], 128), BF16)
        first[k][pairs] = blank
        for s in got[k]:
            got[k][s][pairs] = blank

    def send(k, s, source, at, count):
        return pltpu.make_async_remote_copy(
            src_ref=source.at[pl.ds(at, count)],
            dst_ref=got[k][s].at[pl.ds(at, count)],
            send_sem=send_sem.at[k, s],
            recv_sem=recv_sem.at[k, s],
            device_id=peer(s),
            device_id_type=MESH,
        )

    def move(k, source, d):
        j = c ^ d
        return pltpu.make_async_remote_copy(
            src_ref=source.at[pl.ds(j * band, band)],
            dst_ref=moved[k].at[pl.ds(c * band, band)],
            send_sem=send_sem.at[k, t_stage],
            recv_sem=recv_sem.at[k, t_stage],
            device_id=(r, j),
            device_id_type=MESH,
        )

    def moved_all(k, source):
        count = pairs - band
        return pltpu.make_async_remote_copy(
            src_ref=source.at[pl.ds(0, count)],
            dst_ref=moved[k].at[pl.ds(0, count)],
            send_sem=send_sem.at[k, t_stage],
            recv_sem=recv_sem.at[k, t_stage],
            device_id=(r, c ^ 1),
            device_id_type=MESH,
        )

    def low(k):
        return lax.broadcasted_iota(jnp.int32, (chunks[k], 128), 1) < 64

    def grouped(body, after=None):
        def step(g, carry):
            at = g * GROUP
            body([at + i for i in range(GROUP)])
            if after is not None:
                after(at)
            return carry

        lax.fori_loop(0, pairs // GROUP, step, 0)

    def leaf_task(k):
        n, half = chunks[k], low(k)

        def body(qs):
            zs = []
            for q in qs:
                both = x[rows(k), pl.ds(pl.multiple_of(q * 256, 256), 256)]
                zs.append(jnp.concatenate([both[:, :128], both[:, 128:]], axis=0))
            ys = wide(zs, [leaf[q] for q in qs], 1)
            for q, y in zip(qs, ys):
                first[k][q] = jnp.where(half, y[:n], y[n:]).astype(BF16)

        grouped(body)

    def level_task(k, l, own, other, result, after):
        n, half = chunks[k], low(k)

        def picked(b):
            p, keep = part[l, b], pat[l, b]
            tile = pairs + keep * ((p >> 1) - pairs)
            turn = 1 - (p & 1)
            return pltpu.roll(other[tile], turn * 64, 1)

        def body(qs):
            zs = []
            for q in qs:
                mine = own[q]
                even = jnp.where(half, mine, picked(2 * q))
                odd = jnp.where(half, pltpu.roll(mine, 64, 1), picked(2 * q + 1))
                zs.append(jnp.concatenate([even, odd], axis=0))
            ys = wide(zs, [mid[l, q] for q in qs], 1)
            for q, y in zip(qs, ys):
                result[q] = jnp.where(half, y[:n], y[n:]).astype(BF16)

        grouped(body, after)

    def root_task(k, source):
        n, half = chunks[k], low(k)

        def body(qs):
            zs = []
            for q in qs:
                mine = source[q]
                none = jnp.zeros_like(mine)
                z = [jnp.where(half, mine, none), jnp.where(half, none, mine)]
                zs.append(jnp.concatenate(z, axis=0))
            ys = wide(zs, [root[q] for q in qs], 0)
            for q, y in zip(qs, ys):
                y = y.astype(BF16)
                at = pl.multiple_of(q * 256, 256)
                out[rows(k), pl.ds(at, 128)] = y[:n]
                out[rows(k), pl.ds(at + 128, 128)] = y[n:]

        grouped(body)

    ready = set()

    def need(name, copy):
        if name not in ready:
            ready.add(name)
            copy().wait()

    greeted = [False]

    def greet():
        if not greeted[0]:
            greeted[0] = True
            pl.semaphore_wait(barrier, row_bits + cols - 1)

    def sender(k, s, source):
        def after(at):
            send(k, s, source, at, GROUP).start()

        return after

    held = {}
    for k, t in order:
        if t == 0:
            for i in bands(k):
                need(("x", i), lambda: x_copy(i))
            need("leaf", lambda: leaf_copy)
            leaf_task(k)
            need(("mid", 0), lambda: mid_copy(0))
            greet()
            level_task(k, 0, first[k], first[k], state[k][0], sender(k, 1, state[k][0]))
            held[k] = state[k][0]
        elif t == t_stage:
            moved_all(k, held[k]).wait_recv()
            held[k] = moved[k]
            send(k, t + 1, moved[k], 0, pairs).start()
        elif t <= levels:
            l = t if t < t_stage else t - 1
            need(("mid", l), lambda: mid_copy(l))
            send(k, t, held[k], 0, pairs).wait_recv()
            result = state[k][l % 2]
            if l >= 2:
                before = l - 1 if l <= t_stage + 1 else l
                if before == t_stage:
                    moved_all(k, result).wait_send()
                else:
                    send(k, before, result, 0, pairs).wait_send()
            if t == t_stage - 1:
                level_task(k, l, held[k], got[k][t], result, None)
                for d in range(1, cols):
                    move(k, result, d).start()
                moved[k][pl.ds(c * band, band)] = result[pl.ds(c * band, band)]
            elif t == levels:
                level_task(k, l, held[k], got[k][t], result, None)
            else:
                level_task(k, l, held[k], got[k][t], result, sender(k, t + 1, result))
            held[k] = result
        else:
            need("root", lambda: root_copy)
            root_task(k, held[k])
    for k in range(n_chunks):
        send(k, t_stage + 1, moved[k], 0, pairs).wait_send()
        send(k, levels, state[k][0], 0, pairs).wait_send()


def per_device(right_sides, leaf_factor, middle_factor, root_factor, partners, pattern):
    row_bits = lax.axis_size("row").bit_length() - 1
    col_bits = lax.axis_size("col").bit_length() - 1
    nrhs = right_sides.shape[0]
    blocks, rank, width = leaf_factor.shape
    pairs, levels = blocks // 2, middle_factor.shape[0]
    chunks = CHUNKS
    t_stage = row_bits + 1
    stages = [s for s in range(1, levels + 1) if s != t_stage]
    tiles = [
        pltpu.VMEM((pairs + 1, n, width), BF16) for n in chunks
    ]
    plain = [pltpu.VMEM((pairs, n, width), BF16) for n in chunks]
    scratch = [
        pltpu.VMEM((nrhs, blocks * width), BF16),
        pltpu.VMEM((pairs, 2 * rank, width), BF16),
        pltpu.VMEM((levels, pairs, 2 * rank, width), BF16),
        pltpu.VMEM((pairs, 2 * rank, width), BF16),
        pltpu.SemaphoreType.DMA((nrhs // 16,)),
        pltpu.SemaphoreType.DMA((levels + 2,)),
        pltpu.SemaphoreType.DMA((len(chunks), levels + 1)),
        pltpu.SemaphoreType.DMA((len(chunks), levels + 1)),
    ]
    scratch += tiles
    for one in plain:
        scratch += [one, one]
    scratch += plain
    for one in tiles:
        scratch += [one] * len(stages)
    order = ORDER
    anywhere = pl.BlockSpec(memory_space=pl.ANY)
    scalars = pl.BlockSpec(memory_space=pltpu.SMEM)
    return pl.pallas_call(
        functools.partial(kernel, row_bits, col_bits, chunks, order),
        out_shape=pltpu.VMEM(right_sides.shape, BF16),
        in_specs=[scalars, scalars] + [anywhere] * 4,
        out_specs=pl.BlockSpec(memory_space=pltpu.VMEM),
        scratch_shapes=scratch,
        compiler_params=pltpu.CompilerParams(
            collective_id=0, has_side_effects=True, vmem_limit_bytes=60 << 20
        ),
    )(
        partners.reshape(levels, blocks),
        pattern.reshape(levels, blocks),
        right_sides,
        leaf_factor.reshape(pairs, 2 * rank, width),
        middle_factor.reshape(levels, pairs, 2 * rank, width),
        root_factor.reshape(pairs, 2 * rank, width),
    )


def solution(mesh):
    in_specs = (
        P(None, ("row", "col")),
        P(("row", "col"), None, None),
        P(None, ("row", "col"), None, None),
        P(("row", "col"), None, None),
        P(None, ("row", "col"), None),
        P(None, ("row", "col"), None),
    )
    out_specs = P(None, ("row", "col"))
    return jax.shard_map(
        per_device, mesh=mesh, in_specs=in_specs, out_specs=out_specs, check_vma=False
    )
```

```python
import functools

import jax
import jax.numpy as jnp
from jax import lax
from jax.experimental import pallas as pl
from jax.experimental.pallas import tpu as pltpu
from jax.sharding import PartitionSpec as P

MESH = pl.DeviceIdType.MESH
BF16, F32 = jnp.bfloat16, jnp.float32
CHUNKS = (8, 8, 16, 16, 8, 8)
GROUP = 32
ORDER = (
    (0, 0), (1, 0), (3, 0), (4, 0), (0, 1), (1, 1), (0, 2), (5, 0),
    (3, 1), (0, 3), (1, 2), (2, 0), (3, 2), (0, 4), (4, 1), (0, 5),
    (1, 3), (5, 1), (0, 6), (3, 3), (1, 4), (4, 2), (0, 7), (1, 5),
    (5, 2), (4, 3), (3, 4), (2, 1), (1, 6), (3, 5), (5, 3), (4, 4),
    (1, 7), (2, 2), (3, 6), (4, 5), (0, 8), (5, 4), (2, 3), (1, 8),
    (5, 5), (4, 6), (0, 9), (3, 7), (2, 4), (1, 9), (2, 5), (4, 7),
    (5, 6), (2, 6), (3, 8), (4, 8), (5, 7), (2, 7), (5, 8), (5, 9),
    (4, 9), (3, 9), (2, 8), (2, 9),
)


def wide(zs, weights, contract):
    out = []
    for i in range(0, len(zs), 2):
        both = jnp.concatenate(weights[i : i + 2], axis=1 - contract)
        y = lax.dot_general(
            jnp.concatenate(zs[i : i + 2], axis=0),
            both,
            (((1,), (contract,)), ((), ())),
            preferred_element_type=F32,
        )
        rows = zs[i].shape[0]
        out += [y[:rows, :128], y[rows:, 128:]]
    return out


def kernel(row_bits, col_bits, chunks, order, *refs):
    refs = list(refs)
    part, pat, x_hbm, leaf_hbm, mid_hbm, root_hbm, out = refs[:7]
    x, leaf, mid, root = refs[7:11]
    x_sem, w_sem, send_sem, recv_sem = refs[11:15]
    rest = iter(refs[15:])
    n_chunks = len(chunks)
    starts = [sum(chunks[:k]) for k in range(n_chunks)]
    levels = row_bits + col_bits + 1
    t_stage = row_bits + 1
    first = [next(rest) for _ in chunks]
    state = [[next(rest), next(rest)] for _ in chunks]
    moved = [next(rest) for _ in chunks]
    got = [
        {s: next(rest) for s in range(1, levels + 1) if s != t_stage} for _ in chunks
    ]
    pairs = leaf.shape[0]
    cols = 1 << col_bits
    band = pairs // cols
    r, c = lax.axis_index("row"), lax.axis_index("col")

    def peer(s):
        if s < t_stage:
            return (r ^ (1 << (s - 1)), c)
        return (r, c ^ (1 << (s - t_stage - 1)))

    def rows(k):
        return pl.ds(starts[k], chunks[k])

    n_bands = sum(chunks) // 16

    def bands(k):
        return range(starts[k] // 16, (starts[k] + chunks[k] - 1) // 16 + 1)

    def x_copy(i):
        at = pl.ds(i * 16, 16)
        return pltpu.make_async_copy(x_hbm.at[at], x.at[at], x_sem.at[i])

    leaf_copy = pltpu.make_async_copy(leaf_hbm, leaf, w_sem.at[levels])
    root_copy = pltpu.make_async_copy(root_hbm, root, w_sem.at[levels + 1])

    def mid_copy(l):
        return pltpu.make_async_copy(mid_hbm.at[l], mid.at[l], w_sem.at[l])

    x_first = order[0][0]
    for i in bands(x_first):
        x_copy(i).start()
    leaf_copy.start()
    mid_copy(0).start()
    for i in range(n_bands):
        if i not in bands(x_first):
            x_copy(i).start()
    for l in range(1, levels):
        mid_copy(l).start()
    root_copy.start()

    barrier = pltpu.get_barrier_semaphore()
    for s in range(1, t_stage):
        pl.semaphore_signal(barrier, inc=1, device_id=peer(s), device_id_type=MESH)
    for d in range(1, cols):
        pl.semaphore_signal(barrier, inc=1, device_id=(r, c ^ d), device_id_type=MESH)

    for k in range(n_chunks):
        blank = jnp.zeros((chunks[k], 128), BF16)
        first[k][pairs] = blank
        for s in got[k]:
            got[k][s][pairs] = blank

    def send(k, s, source, at, count):
        return pltpu.make_async_remote_copy(
            src_ref=source.at[pl.ds(at, count)],
            dst_ref=got[k][s].at[pl.ds(at, count)],
            send_sem=send_sem.at[k, s],
            recv_sem=recv_sem.at[k, s],
            device_id=peer(s),
            device_id_type=MESH,
        )

    def move(k, source, d):
        j = c ^ d
        return pltpu.make_async_remote_copy(
            src_ref=source.at[pl.ds(j * band, band)],
            dst_ref=moved[k].at[pl.ds(c * band, band)],
            send_sem=send_sem.at[k, t_stage],
            recv_sem=recv_sem.at[k, t_stage],
            device_id=(r, j),
            device_id_type=MESH,
        )

    def moved_all(k, source):
        count = pairs - band
        return pltpu.make_async_remote_copy(
            src_ref=source.at[pl.ds(0, count)],
            dst_ref=moved[k].at[pl.ds(0, count)],
            send_sem=send_sem.at[k, t_stage],
            recv_sem=recv_sem.at[k, t_stage],
            device_id=(r, c ^ 1),
            device_id_type=MESH,
        )

    def low(k):
        return lax.broadcasted_iota(jnp.int32, (chunks[k], 128), 1) < 64

    def grouped(body, after=None):
        def step(g, carry):
            at = g * GROUP
            body([at + i for i in range(GROUP)])
            if after is not None:
                after(at)
            return carry

        lax.fori_loop(0, pairs // GROUP, step, 0)

    def leaf_task(k):
        n, half = chunks[k], low(k)

        def body(qs):
            zs = []
            for q in qs:
                both = x[rows(k), pl.ds(pl.multiple_of(q * 256, 256), 256)]
                zs.append(jnp.concatenate([both[:, :128], both[:, 128:]], axis=0))
            ys = wide(zs, [leaf[q] for q in qs], 1)
            for q, y in zip(qs, ys):
                first[k][q] = jnp.where(half, y[:n], y[n:]).astype(BF16)

        grouped(body)

    def level_task(k, l, own, other, result, after):
        n, half = chunks[k], low(k)

        def picked(b):
            p, keep = part[l, b], pat[l, b]
            tile = pairs + keep * ((p >> 1) - pairs)
            turn = 1 - (p & 1)
            return pltpu.roll(other[tile], turn * 64, 1)

        def body(qs):
            zs = []
            for q in qs:
                mine = own[q]
                even = jnp.where(half, mine, picked(2 * q))
                odd = jnp.where(half, pltpu.roll(mine, 64, 1), picked(2 * q + 1))
                zs.append(jnp.concatenate([even, odd], axis=0))
            ys = wide(zs, [mid[l, q] for q in qs], 1)
            for q, y in zip(qs, ys):
                result[q] = jnp.where(half, y[:n], y[n:]).astype(BF16)

        grouped(body, after)

    def root_task(k, source):
        n, half = chunks[k], low(k)

        def body(qs):
            zs = []
            for q in qs:
                mine = source[q]
                none = jnp.zeros_like(mine)
                z = [jnp.where(half, mine, none), jnp.where(half, none, mine)]
                zs.append(jnp.concatenate(z, axis=0))
            ys = wide(zs, [root[q] for q in qs], 0)
            for q, y in zip(qs, ys):
                y = y.astype(BF16)
                at = pl.multiple_of(q * 256, 256)
                out[rows(k), pl.ds(at, 128)] = y[:n]
                out[rows(k), pl.ds(at + 128, 128)] = y[n:]

        grouped(body)

    ready = set()

    def need(name, copy):
        if name not in ready:
            ready.add(name)
            copy().wait()

    greeted = [False]

    def greet():
        if not greeted[0]:
            greeted[0] = True
            pl.semaphore_wait(barrier, row_bits + cols - 1)

    def sender(k, s, source):
        def after(at):
            send(k, s, source, at, GROUP).start()

        return after

    held = {}
    for k, t in order:
        if t == 0:
            for i in bands(k):
                need(("x", i), lambda: x_copy(i))
            need("leaf", lambda: leaf_copy)
            leaf_task(k)
            need(("mid", 0), lambda: mid_copy(0))
            greet()
            level_task(k, 0, first[k], first[k], state[k][0], sender(k, 1, state[k][0]))
            held[k] = state[k][0]
        elif t == t_stage:
            moved_all(k, held[k]).wait_recv()
            held[k] = moved[k]
            send(k, t + 1, moved[k], 0, pairs).start()
        elif t <= levels:
            l = t if t < t_stage else t - 1
            need(("mid", l), lambda: mid_copy(l))
            send(k, t, held[k], 0, pairs).wait_recv()
            result = state[k][l % 2]
            if l >= 2:
                before = l - 1 if l <= t_stage + 1 else l
                if before == t_stage:
                    moved_all(k, result).wait_send()
                else:
                    send(k, before, result, 0, pairs).wait_send()
            if t == t_stage - 1:
                level_task(k, l, held[k], got[k][t], result, None)
                for d in range(1, cols):
                    move(k, result, d).start()
                moved[k][pl.ds(c * band, band)] = result[pl.ds(c * band, band)]
            elif t == levels:
                level_task(k, l, held[k], got[k][t], result, None)
            else:
                level_task(k, l, held[k], got[k][t], result, sender(k, t + 1, result))
            held[k] = result
        else:
            need("root", lambda: root_copy)
            root_task(k, held[k])
    for k in range(n_chunks):
        send(k, t_stage + 1, moved[k], 0, pairs).wait_send()
        send(k, levels, state[k][0], 0, pairs).wait_send()


def per_device(right_sides, leaf_factor, middle_factor, root_factor, partners, pattern):
    row_bits = lax.axis_size("row").bit_length() - 1
    col_bits = lax.axis_size("col").bit_length() - 1
    nrhs = right_sides.shape[0]
    blocks, rank, width = leaf_factor.shape
    pairs, levels = blocks // 2, middle_factor.shape[0]
    chunks = CHUNKS
    t_stage = row_bits + 1
    stages = [s for s in range(1, levels + 1) if s != t_stage]
    tiles = [
        pltpu.VMEM((pairs + 1, n, width), BF16) for n in chunks
    ]
    plain = [pltpu.VMEM((pairs, n, width), BF16) for n in chunks]
    scratch = [
        pltpu.VMEM((nrhs, blocks * width), BF16),
        pltpu.VMEM((pairs, 2 * rank, width), BF16),
        pltpu.VMEM((levels, pairs, 2 * rank, width), BF16),
        pltpu.VMEM((pairs, 2 * rank, width), BF16),
        pltpu.SemaphoreType.DMA((nrhs // 16,)),
        pltpu.SemaphoreType.DMA((levels + 2,)),
        pltpu.SemaphoreType.DMA((len(chunks), levels + 1)),
        pltpu.SemaphoreType.DMA((len(chunks), levels + 1)),
    ]
    scratch += tiles
    for one in plain:
        scratch += [one, one]
    scratch += plain
    for one in tiles:
        scratch += [one] * len(stages)
    order = ORDER
    anywhere = pl.BlockSpec(memory_space=pl.ANY)
    scalars = pl.BlockSpec(memory_space=pltpu.SMEM)
    return pl.pallas_call(
        functools.partial(kernel, row_bits, col_bits, chunks, order),
        out_shape=pltpu.VMEM(right_sides.shape, BF16),
        in_specs=[scalars, scalars] + [anywhere] * 4,
        out_specs=pl.BlockSpec(memory_space=pltpu.VMEM),
        scratch_shapes=scratch,
        compiler_params=pltpu.CompilerParams(
            collective_id=0, has_side_effects=True, vmem_limit_bytes=60 << 20
        ),
    )(
        partners.reshape(levels, blocks),
        pattern.reshape(levels, blocks),
        right_sides,
        leaf_factor.reshape(pairs, 2 * rank, width),
        middle_factor.reshape(levels, pairs, 2 * rank, width),
        root_factor.reshape(pairs, 2 * rank, width),
    )


def solution(mesh):
    in_specs = (
        P(None, ("row", "col")),
        P(("row", "col"), None, None),
        P(None, ("row", "col"), None, None),
        P(("row", "col"), None, None),
        P(None, ("row", "col"), None),
        P(None, ("row", "col"), None),
    )
    out_specs = P(None, ("row", "col"))
    return jax.shard_map(
        per_device, mesh=mesh, in_specs=in_specs, out_specs=out_specs, check_vma=False
    )
```

```python
import functools

import jax
import jax.numpy as jnp
from jax import lax
from jax.experimental import pallas as pl
from jax.experimental.pallas import tpu as pltpu
from jax.sharding import PartitionSpec as P

MESH = pl.DeviceIdType.MESH
BF16, F32 = jnp.bfloat16, jnp.float32
CHUNKS = (8, 8, 16, 16, 8, 8)
GROUP = 32
ORDER = (
    (0, 0), (1, 0), (3, 0), (4, 0), (0, 1), (1, 1), (0, 2), (5, 0),
    (3, 1), (0, 3), (1, 2), (2, 0), (3, 2), (0, 4), (4, 1), (0, 5),
    (1, 3), (5, 1), (0, 6), (3, 3), (1, 4), (4, 2), (0, 7), (1, 5),
    (5, 2), (4, 3), (3, 4), (2, 1), (1, 6), (3, 5), (5, 3), (4, 4),
    (1, 7), (2, 2), (3, 6), (4, 5), (0, 8), (5, 4), (2, 3), (1, 8),
    (5, 5), (4, 6), (0, 9), (3, 7), (2, 4), (1, 9), (2, 5), (4, 7),
    (5, 6), (2, 6), (3, 8), (4, 8), (5, 7), (2, 7), (5, 8), (5, 9),
    (4, 9), (3, 9), (2, 8), (2, 9),
)


def wide(zs, weights, contract):
    out = []
    for i in range(0, len(zs), 2):
        both = jnp.concatenate(weights[i : i + 2], axis=1 - contract)
        y = lax.dot_general(
            jnp.concatenate(zs[i : i + 2], axis=0),
            both,
            (((1,), (contract,)), ((), ())),
            preferred_element_type=F32,
        )
        rows = zs[i].shape[0]
        out += [y[:rows, :128], y[rows:, 128:]]
    return out


def kernel(row_bits, col_bits, chunks, order, *refs):
    refs = list(refs)
    part, pat, x_hbm, leaf_hbm, mid_hbm, root_hbm, out = refs[:7]
    x, leaf, mid, root = refs[7:11]
    x_sem, w_sem, send_sem, recv_sem = refs[11:15]
    rest = iter(refs[15:])
    n_chunks = len(chunks)
    starts = [sum(chunks[:k]) for k in range(n_chunks)]
    levels = row_bits + col_bits + 1
    t_stage = row_bits + 1
    first = [next(rest) for _ in chunks]
    state = [[next(rest), next(rest)] for _ in chunks]
    moved = [next(rest) for _ in chunks]
    got = [
        {s: next(rest) for s in range(1, levels + 1) if s != t_stage} for _ in chunks
    ]
    pairs = leaf.shape[0]
    cols = 1 << col_bits
    band = pairs // cols
    r, c = lax.axis_index("row"), lax.axis_index("col")

    def peer(s):
        if s < t_stage:
            return (r ^ (1 << (s - 1)), c)
        return (r, c ^ (1 << (s - t_stage - 1)))

    def rows(k):
        return pl.ds(starts[k], chunks[k])

    n_bands = sum(chunks) // 16

    def bands(k):
        return range(starts[k] // 16, (starts[k] + chunks[k] - 1) // 16 + 1)

    def x_copy(i):
        at = pl.ds(i * 16, 16)
        return pltpu.make_async_copy(x_hbm.at[at], x.at[at], x_sem.at[i])

    leaf_copy = pltpu.make_async_copy(leaf_hbm, leaf, w_sem.at[levels])
    root_copy = pltpu.make_async_copy(root_hbm, root, w_sem.at[levels + 1])

    def mid_copy(l):
        return pltpu.make_async_copy(mid_hbm.at[l], mid.at[l], w_sem.at[l])

    x_first = order[0][0]
    for i in bands(x_first):
        x_copy(i).start()
    leaf_copy.start()
    mid_copy(0).start()
    barrier = pltpu.get_barrier_semaphore()
    for s in range(1, t_stage):
        pl.semaphore_signal(barrier, inc=1, device_id=peer(s), device_id_type=MESH)
    for d in range(1, cols):
        pl.semaphore_signal(barrier, inc=1, device_id=(r, c ^ d), device_id_type=MESH)

    for i in range(n_bands):
        if i not in bands(x_first):
            x_copy(i).start()
    for l in range(1, levels):
        mid_copy(l).start()
    root_copy.start()

    for k in range(n_chunks):
        blank = jnp.zeros((chunks[k], 128), BF16)
        first[k][pairs] = blank
        for s in got[k]:
            got[k][s][pairs] = blank

    def send(k, s, source, at, count):
        return pltpu.make_async_remote_copy(
            src_ref=source.at[pl.ds(at, count)],
            dst_ref=got[k][s].at[pl.ds(at, count)],
            send_sem=send_sem.at[k, s],
            recv_sem=recv_sem.at[k, s],
            device_id=peer(s),
            device_id_type=MESH,
        )

    def move(k, source, d):
        j = c ^ d
        return pltpu.make_async_remote_copy(
            src_ref=source.at[pl.ds(j * band, band)],
            dst_ref=moved[k].at[pl.ds(c * band, band)],
            send_sem=send_sem.at[k, t_stage],
            recv_sem=recv_sem.at[k, t_stage],
            device_id=(r, j),
            device_id_type=MESH,
        )

    def moved_all(k, source):
        count = pairs - band
        return pltpu.make_async_remote_copy(
            src_ref=source.at[pl.ds(0, count)],
            dst_ref=moved[k].at[pl.ds(0, count)],
            send_sem=send_sem.at[k, t_stage],
            recv_sem=recv_sem.at[k, t_stage],
            device_id=(r, c ^ 1),
            device_id_type=MESH,
        )

    def low(k):
        return lax.broadcasted_iota(jnp.int32, (chunks[k], 128), 1) < 64

    def grouped(body, after=None):
        def step(g, carry):
            at = g * GROUP
            body([at + i for i in range(GROUP)])
            if after is not None:
                after(at)
            return carry

        lax.fori_loop(0, pairs // GROUP, step, 0)

    def leaf_task(k):
        n, half = chunks[k], low(k)

        def body(qs):
            zs = []
            for q in qs:
                both = x[rows(k), pl.ds(pl.multiple_of(q * 256, 256), 256)]
                zs.append(jnp.concatenate([both[:, :128], both[:, 128:]], axis=0))
            ys = wide(zs, [leaf[q] for q in qs], 1)
            for q, y in zip(qs, ys):
                first[k][q] = jnp.where(half, y[:n], y[n:]).astype(BF16)

        grouped(body)

    def level_task(k, l, own, other, result, after):
        n, half = chunks[k], low(k)

        def picked(b):
            p, keep = part[l, b], pat[l, b]
            tile = pairs + keep * ((p >> 1) - pairs)
            turn = 1 - (p & 1)
            return pltpu.roll(other[tile], turn * 64, 1)

        def body(qs):
            zs = []
            for q in qs:
                mine = own[q]
                even = jnp.where(half, mine, picked(2 * q))
                odd = jnp.where(half, pltpu.roll(mine, 64, 1), picked(2 * q + 1))
                zs.append(jnp.concatenate([even, odd], axis=0))
            ys = wide(zs, [mid[l, q] for q in qs], 1)
            for q, y in zip(qs, ys):
                result[q] = jnp.where(half, y[:n], y[n:]).astype(BF16)

        grouped(body, after)

    def root_task(k, source):
        n, half = chunks[k], low(k)

        def body(qs):
            zs = []
            for q in qs:
                mine = source[q]
                none = jnp.zeros_like(mine)
                z = [jnp.where(half, mine, none), jnp.where(half, none, mine)]
                zs.append(jnp.concatenate(z, axis=0))
            ys = wide(zs, [root[q] for q in qs], 0)
            for q, y in zip(qs, ys):
                y = y.astype(BF16)
                at = pl.multiple_of(q * 256, 256)
                out[rows(k), pl.ds(at, 128)] = y[:n]
                out[rows(k), pl.ds(at + 128, 128)] = y[n:]

        grouped(body)

    ready = set()

    def need(name, copy):
        if name not in ready:
            ready.add(name)
            copy().wait()

    greeted = [False]

    def greet():
        if not greeted[0]:
            greeted[0] = True
            pl.semaphore_wait(barrier, row_bits + cols - 1)

    def sender(k, s, source):
        def after(at):
            send(k, s, source, at, GROUP).start()

        return after

    held = {}
    for k, t in order:
        if t == 0:
            for i in bands(k):
                need(("x", i), lambda: x_copy(i))
            need("leaf", lambda: leaf_copy)
            leaf_task(k)
            need(("mid", 0), lambda: mid_copy(0))
            greet()
            level_task(k, 0, first[k], first[k], state[k][0], sender(k, 1, state[k][0]))
            held[k] = state[k][0]
        elif t == t_stage:
            moved_all(k, held[k]).wait_recv()
            held[k] = moved[k]
            send(k, t + 1, moved[k], 0, pairs).start()
        elif t <= levels:
            l = t if t < t_stage else t - 1
            need(("mid", l), lambda: mid_copy(l))
            send(k, t, held[k], 0, pairs).wait_recv()
            result = state[k][l % 2]
            if l >= 2:
                before = l - 1 if l <= t_stage + 1 else l
                if before == t_stage:
                    moved_all(k, result).wait_send()
                else:
                    send(k, before, result, 0, pairs).wait_send()
            if t == t_stage - 1:
                level_task(k, l, held[k], got[k][t], result, None)
                for d in range(1, cols):
                    move(k, result, d).start()
                moved[k][pl.ds(c * band, band)] = result[pl.ds(c * band, band)]
            elif t == levels:
                level_task(k, l, held[k], got[k][t], result, None)
            else:
                level_task(k, l, held[k], got[k][t], result, sender(k, t + 1, result))
            held[k] = result
        else:
            need("root", lambda: root_copy)
            root_task(k, held[k])
    for k in range(n_chunks):
        send(k, t_stage + 1, moved[k], 0, pairs).wait_send()
        send(k, levels, state[k][0], 0, pairs).wait_send()


def per_device(right_sides, leaf_factor, middle_factor, root_factor, partners, pattern):
    row_bits = lax.axis_size("row").bit_length() - 1
    col_bits = lax.axis_size("col").bit_length() - 1
    nrhs = right_sides.shape[0]
    blocks, rank, width = leaf_factor.shape
    pairs, levels = blocks // 2, middle_factor.shape[0]
    chunks = CHUNKS
    t_stage = row_bits + 1
    stages = [s for s in range(1, levels + 1) if s != t_stage]
    tiles = [
        pltpu.VMEM((pairs + 1, n, width), BF16) for n in chunks
    ]
    plain = [pltpu.VMEM((pairs, n, width), BF16) for n in chunks]
    scratch = [
        pltpu.VMEM((nrhs, blocks * width), BF16),
        pltpu.VMEM((pairs, 2 * rank, width), BF16),
        pltpu.VMEM((levels, pairs, 2 * rank, width), BF16),
        pltpu.VMEM((pairs, 2 * rank, width), BF16),
        pltpu.SemaphoreType.DMA((nrhs // 16,)),
        pltpu.SemaphoreType.DMA((levels + 2,)),
        pltpu.SemaphoreType.DMA((len(chunks), levels + 1)),
        pltpu.SemaphoreType.DMA((len(chunks), levels + 1)),
    ]
    scratch += tiles
    for one in plain:
        scratch += [one, one]
    scratch += plain
    for one in tiles:
        scratch += [one] * len(stages)
    order = ORDER
    anywhere = pl.BlockSpec(memory_space=pl.ANY)
    scalars = pl.BlockSpec(memory_space=pltpu.SMEM)
    return pl.pallas_call(
        functools.partial(kernel, row_bits, col_bits, chunks, order),
        out_shape=pltpu.VMEM(right_sides.shape, BF16),
        in_specs=[scalars, scalars] + [anywhere] * 4,
        out_specs=pl.BlockSpec(memory_space=pltpu.VMEM),
        scratch_shapes=scratch,
        compiler_params=pltpu.CompilerParams(
            collective_id=0, has_side_effects=True, vmem_limit_bytes=60 << 20
        ),
    )(
        partners.reshape(levels, blocks),
        pattern.reshape(levels, blocks),
        right_sides,
        leaf_factor.reshape(pairs, 2 * rank, width),
        middle_factor.reshape(levels, pairs, 2 * rank, width),
        root_factor.reshape(pairs, 2 * rank, width),
    )


def solution(mesh):
    in_specs = (
        P(None, ("row", "col")),
        P(("row", "col"), None, None),
        P(None, ("row", "col"), None, None),
        P(("row", "col"), None, None),
        P(None, ("row", "col"), None),
        P(None, ("row", "col"), None),
    )
    out_specs = P(None, ("row", "col"))
    return jax.shard_map(
        per_device, mesh=mesh, in_specs=in_specs, out_specs=out_specs, check_vma=False
    )
```
